768 devices in a mesh: dp: 96 (over z, y_lo, x), mp: 8 (over y_hi, core).
Axes of the slice: x: 4, y: 8 (y_hi: 4, y_lo: 2; y = y_hi * 2 + y_lo), z: 12, core: 2. Of those that a mesh axis runs over, the one named last changes fastest.
Arguments:
- tokens: bfloat16 [49152, 3072], P(('dp', 'mp')), parts along dimension 0, may hold values from -6 to 6
- ln_gain: float32 [3072], replicated, may hold values from 0.5 to 1.5
- w_in: bfloat16 [3072, 9216], P(None, 'mp'), may hold values from -0.108253175 to 0.108253175
- qk_gain: float32 [2, 24, 128], P(None, 'mp'), may hold values from 0.45 to 6
- w_out: bfloat16 [3072, 3072], P('mp'), may hold values from -0.109375 to 0.109375
Outputs:
- block_out: bfloat16 [49152, 3072], P(('dp', 'mp')), parts along dimension 0
The draws below stay inside these ranges and needn't reach their ends.
There are 96 independent parts, one for each index of `dp`. The reference program is written for one: setup_inputs(seed, part) draws one part's arguments, and reference() takes and returns one part's arrays. A program takes and returns all parts, laid end to end along the dimension named above; an argument that names none is the same for every part. Nothing has to cross between parts.
All inputs are finite; a program needn't handle non-finite values.
Results may differ from the reference program's by a relative error of at most 0.015.
Values may be sent and summed in bfloat16 or wider, within the bound.
No kernel may reach another device: no remote copies, remote signals or barrier semaphores. Data moves between devices by JAX's collectives and lax.ppermute only.
A program may use at most 32 MiB of HBM per device.

```python
import math
import jax
import jax.numpy as jnp
from jax import lax

D = 3072
HEAD = 128
HEADS_DEV = 3
PATCHES = 256
HEADS = 24
TOKENS = 512
IN_COLS = 9216
OUT_ROWS = 3072
N_MP = 8


def draw_w_in(key, part):
    key = jax.random.fold_in(key, 11)
    head_cols = HEADS_DEV * HEAD
    group_cols = 3 * head_cols
    groups = IN_COLS // group_cols
    columns = jnp.clip(jax.random.normal(key, (D, groups, group_cols), jnp.float32), -6.0, 6.0)
    return (columns / math.sqrt(D)).reshape(D, IN_COLS).astype(jnp.bfloat16)


def draw_qk_gain(key, part):
    key = jax.random.fold_in(key, 12)
    scale_key, noise_key = jax.random.split(key)
    noise = jnp.clip(jax.random.normal(noise_key, (2, HEADS, HEAD), jnp.float32), -3.0, 3.0)
    scale = jnp.exp(jax.random.uniform(scale_key, (1, HEADS, 1), jnp.float32, math.log(0.7), math.log(2.0)))
    return scale * (1.0 + 0.1 * noise)


def level_of(stream_key, shape, shards, least, top_value):
    loudness = 1.0
    for dim, blocks in shards:
        draws = jax.random.uniform(jax.random.fold_in(jax.random.fold_in(stream_key, 6), dim), (blocks,), jnp.float32, least / len(shards), top_value / len(shards))
        loudness = loudness * jnp.repeat(jnp.exp(draws), shape[dim] // blocks).reshape((-1,) + (1,) * (len(shape) - 1 - dim))
    return loudness


def scatter_about(key, shape, scale, limit, pieces=(), kind=jnp.bfloat16):
    drawn = jax.random.normal(key, shape, jnp.float32) * scale
    if len(pieces) > 0:
        drawn = level_of(key, shape, pieces, -0.22, 0.18) * drawn
    return jnp.clip(drawn, min=-limit, max=limit).astype(kind)


def setup_inputs(seed: int = 0, part: int = 0) -> dict:
    splits = jax.random.split(jax.random.key(seed), 6)
    own_keys = jax.random.split(jax.random.fold_in(splits[5], part), 6)
    return {
        "tokens": scatter_about(own_keys[0], (TOKENS, D), 1.0, 6.0, ((0, 8),)),
        "ln_gain": jnp.clip(1.0 + 0.1 * jax.random.normal(splits[1], (D,), jnp.float32), 0.5, 1.5),
        "w_in": draw_w_in(jax.random.fold_in(splits[5], 71), part),
        "qk_gain": draw_qk_gain(jax.random.fold_in(splits[5], 71), part),
        "w_out": scatter_about(splits[4], (OUT_ROWS, D), OUT_ROWS ** -0.5, 0.109375, ((0, 8),)),
    }


EPSILON = 1e-06

def layer_norm(entries, gain_row):
    average = lax.optimization_barrier(jnp.mean(entries, axis=-1, keepdims=True))
    centred = entries - average
    spread = lax.optimization_barrier(jnp.mean(centred * centred, axis=-1, keepdims=True))
    return centred * lax.rsqrt(spread + EPSILON) * gain_row

def attend(queries, key_rows, value_rows):
    images = queries.shape[0] // PATCHES
    left = queries.astype(jnp.float32).reshape(images, PATCHES, -1, HEAD)
    right = key_rows.astype(jnp.float32).reshape(images, PATCHES, -1, HEAD)
    carried = value_rows.astype(jnp.float32).reshape(images, PATCHES, -1, HEAD)
    scores = jnp.einsum('iphd,iqhd->ihpq', left, right) / math.sqrt(HEAD)
    largest = lax.optimization_barrier(jnp.max(scores, axis=-1, keepdims=True))
    raised = jnp.exp(scores - largest)
    denominator = lax.optimization_barrier(jnp.sum(raised, axis=-1, keepdims=True))
    weights = (raised / denominator).astype(jnp.bfloat16)
    mixed = jnp.einsum('ihpq,iqhd->iphd', weights.astype(jnp.float32), carried)
    return mixed.reshape(queries.shape[0], -1, HEAD).astype(jnp.bfloat16)

def reference(tokens, ln_gain, w_in, qk_gain, w_out):
    head_cols = HEADS_DEV * HEAD
    group_cols = 3 * head_cols
    normed = layer_norm(tokens.astype(jnp.float32), ln_gain.astype(jnp.float32)).astype(jnp.bfloat16)
    projected = jnp.dot(normed, w_in, preferred_element_type=jnp.float32).reshape(TOKENS, N_MP, group_cols)
    queries = projected[:, :, :head_cols].reshape(TOKENS, HEADS, HEAD)
    key_rows = projected[:, :, head_cols:2 * head_cols].reshape(TOKENS, HEADS, HEAD)
    value_rows = projected[:, :, 2 * head_cols:3 * head_cols].reshape(TOKENS, HEADS, HEAD).astype(jnp.bfloat16)
    queries = layer_norm(queries, qk_gain[0]).astype(jnp.bfloat16)
    key_rows = layer_norm(key_rows, qk_gain[1]).astype(jnp.bfloat16)
    attended = attend(queries, key_rows, value_rows)
    joined = attended.reshape(TOKENS, N_MP, head_cols)
    branch = jnp.zeros((TOKENS, D), jnp.float32)
    for group in range(N_MP):
        weight_rows = w_out[group * head_cols:(group + 1) * head_cols]
        term = jnp.dot(joined[:, group, :], weight_rows, preferred_element_type=jnp.float32).astype(jnp.bfloat16)
        branch = branch + term.astype(jnp.float32)
    return (tokens.astype(jnp.float32) + branch).astype(jnp.bfloat16)
```

```python
import math

import jax
import jax.numpy as jnp
from jax import lax
from jax.experimental import pallas as pl
from jax.experimental.pallas import tpu as pltpu
from jax.sharding import PartitionSpec as P

EPSILON = 1e-06
CHIPS = 4
CORES = 2


def place(chip, core):
    return (chip % CHIPS) * CORES + core


NEAR_A = [
    (place(0, 0), place(1, 0)), (place(0, 1), place(3, 0)), (place(1, 0), place(0, 0)), (place(1, 1), place(2, 0)),
    (place(2, 0), place(3, 1)), (place(2, 1), place(1, 1)), (place(3, 0), place(2, 1)), (place(3, 1), place(0, 1)),
]
NEAR_B = [
    (place(0, 0), place(3, 0)), (place(0, 1), place(1, 0)), (place(1, 0), place(2, 0)), (place(1, 1), place(0, 0)),
    (place(2, 0), place(1, 1)), (place(2, 1), place(3, 1)), (place(3, 0), place(0, 1)), (place(3, 1), place(2, 1)),
]
SAME = [(place(0, 1), place(0, 0)), (place(1, 1), place(1, 0)), (place(2, 0), place(2, 1)), (place(3, 0), place(3, 1))]
FAR_A = [(place(1, 0), place(2, 0)), (place(0, 0), place(3, 0)), (place(3, 1), place(0, 1)), (place(2, 1), place(1, 1))]
FAR_B = [(place(3, 0), place(2, 0)), (place(2, 0), place(3, 0)), (place(1, 1), place(0, 1)), (place(0, 1), place(1, 1))]
SWAP = [(i, i ^ 1) for i in range(CHIPS * CORES)]


def back(pairs):
    return [(target, source) for source, target in pairs]


def send(value, pairs):
    return lax.ppermute(value, "mp", pairs)


def normalize(entries, gain):
    average = jnp.mean(entries, axis=-1, keepdims=True)
    centred = entries - average
    spread = jnp.mean(centred * centred, axis=-1, keepdims=True)
    return centred * lax.rsqrt(spread + EPSILON) * gain


def norm_rows(ref, gain_ref, normed, at):
    step = 16

    @pl.loop(0, ref.shape[0] // step)
    def _(i):
        entries = ref[pl.ds(pl.multiple_of(i * step, step), step), :].astype(jnp.float32)
        normed[pl.ds(pl.multiple_of(at + i * step, step), step), :] = normalize(entries, gain_ref[...]).astype(
            jnp.bfloat16
        )


def project(normed, w_ref, projected, top, left):
    rows, width = normed.shape[0], w_ref.shape[1]
    for start in range(0, width, 256):
        size = min(256, width - start)
        projected[top : top + rows, left + start : left + start + size] = jnp.dot(
            normed[...], w_ref[:, start : start + size], preferred_element_type=jnp.float32
        )


def out_terms(joined, w_ref, w2_ref, upper_ref, lower_ref):
    half, block = w_ref.shape[0], upper_ref.shape[0]
    for start in range(0, upper_ref.shape[1], 512):
        columns = slice(start, start + 512)
        term = jnp.dot(joined[:, :half], w_ref[:, columns], preferred_element_type=jnp.float32) + jnp.dot(
            joined[:, half:], w2_ref[:, columns], preferred_element_type=jnp.float32
        )
        upper_ref[:, columns] = term[:block].astype(jnp.bfloat16)
        lower_ref[:, columns] = term[block:].astype(jnp.bfloat16)


def near_kernel(a_ref, b_ref, gain_ref, w_hbm, w2_hbm, wo_hbm, wo2_hbm, w_ref, w2_ref, wo_ref, wo2_ref, projected, normed, sems):
    loads = [
        pltpu.make_async_copy(source, target, sems.at[i])
        for i, (source, target) in enumerate(((w_hbm, w_ref), (w2_hbm, w2_ref), (wo_hbm, wo_ref), (wo2_hbm, wo2_ref)))
    ]
    for load in loads:
        load.start()
    norm_rows(a_ref, gain_ref, normed, 0)
    norm_rows(b_ref, gain_ref, normed, a_ref.shape[0])
    loads[0].wait()
    project(normed, w_ref, projected, 0, 0)
    loads[1].wait()
    project(normed, w2_ref, projected, 0, w_ref.shape[1])
    loads[2].wait()
    loads[3].wait()


def attention_kernel(
    local_ref, own_ref, same_ref, far_a_ref, far_b_ref, gain_ref, qk_ref, qk2_ref, w_ref, w2_ref, wo_ref, wo2_ref,
    near_ref, joined_ref, third_ref, fourth_ref, normed, projected, joined,
):
    block = own_ref.shape[0]
    heads, head_size = qk_ref.shape[1:]

    @pl.when(local_ref[0] == 1)
    def _():
        norm_rows(same_ref, gain_ref, normed, 0)
        norm_rows(own_ref, gain_ref, normed, block)

    @pl.when(local_ref[0] == 0)
    def _():
        norm_rows(far_a_ref, gain_ref, normed, 0)
        norm_rows(far_b_ref, gain_ref, normed, block)

    width = w_ref.shape[1]
    project(normed, w_ref, projected, 0, 0)
    project(normed, w2_ref, projected, 0, width)

    for index, ref in ((0, qk_ref), (1, qk2_ref)):
        for head in range(heads):
            def part(kind):
                at = index * width + (kind * heads + head) * head_size
                return jnp.concatenate([near_ref[:, at : at + head_size], projected[:, at : at + head_size]], axis=0)

            queries = normalize(part(0), ref[0, head : head + 1, :]).astype(jnp.bfloat16)
            keys = normalize(part(1), ref[1, head : head + 1, :]).astype(jnp.bfloat16)
            values = part(2).astype(jnp.bfloat16)
            scores = lax.dot_general(
                queries, keys, (((1,), (1,)), ((), ())), preferred_element_type=jnp.float32
            ) * (1.0 / math.sqrt(head_size))
            raised = jnp.exp(scores - jnp.max(scores, axis=-1, keepdims=True))
            weights = (raised * (1.0 / jnp.sum(raised, axis=-1, keepdims=True))).astype(jnp.bfloat16)
            mixed = jnp.dot(weights, values, preferred_element_type=jnp.float32).astype(jnp.bfloat16)
            at = (index * heads + head) * head_size
            joined_ref[:, at : at + head_size] = mixed[: 2 * block]
            joined[:, at : at + head_size] = mixed[2 * block :]

    out_terms(joined, wo_ref, wo2_ref, third_ref, fourth_ref)


def output_kernel(joined_ref, wo_ref, wo2_ref, first_ref, second_ref):
    out_terms(joined_ref, wo_ref, wo2_ref, first_ref, second_ref)


def whole(count, space=pltpu.VMEM):
    return [pl.BlockSpec(memory_space=space)] * count


def held(value):
    return pltpu.with_memory_space_constraint(value, pltpu.VMEM)


def stored(value):
    return pltpu.with_memory_space_constraint(value, pltpu.HBM)


def body(tokens, ln_gain, w_in, qk_gain, w_out):
    block, width = tokens.shape
    heads, head_size = qk_gain.shape[1:]
    me = lax.axis_index("mp")
    local = (me // (CHIPS // 2 * CORES)) == (me % CORES)
    gain = ln_gain.reshape(1, width)

    near_a = send(tokens, NEAR_A)
    near_b = send(tokens, NEAR_B)
    w_in2 = send(w_in, SWAP)
    w_out2 = send(w_out, SWAP)
    qk_gain2 = send(qk_gain, SWAP)
    same = send(tokens, SAME)
    far_a = send(near_a, FAR_A)
    far_b = send(near_a, FAR_B)

    row_block = jax.ShapeDtypeStruct((block, width), jnp.bfloat16)
    w_vmem, w2_vmem, wo_vmem, wo2_vmem, projected = pl.pallas_call(
        near_kernel,
        out_shape=(
            pltpu.VMEM(w_in.shape, jnp.bfloat16),
            pltpu.VMEM(w_in.shape, jnp.bfloat16),
            pltpu.VMEM(w_out.shape, jnp.bfloat16),
            pltpu.VMEM(w_out.shape, jnp.bfloat16),
            pltpu.VMEM((2 * block, 2 * w_in.shape[1]), jnp.float32),
        ),
        in_specs=whole(3) + whole(4, pl.ANY),
        out_specs=tuple(whole(5)),
        scratch_shapes=[pltpu.VMEM((2 * block, width), jnp.bfloat16), pltpu.SemaphoreType.DMA((4,))],
        compiler_params=pltpu.CompilerParams(vmem_limit_bytes=12 * 1024 * 1024),
        cost_estimate=pl.CostEstimate(flops=2_000_000_000, bytes_accessed=19_000_000, transcendentals=0),
    )(stored(near_a), stored(near_b), gain, stored(w_in), stored(w_in2), stored(w_out), stored(w_out2))
    w_vmem, w2_vmem, wo_vmem, wo2_vmem, projected = (
        held(value) for value in (w_vmem, w2_vmem, wo_vmem, wo2_vmem, projected)
    )
    joined, third, fourth = pl.pallas_call(
        attention_kernel,
        out_shape=(jax.ShapeDtypeStruct((2 * block, 2 * heads * head_size), jnp.bfloat16), row_block, row_block),
        in_specs=whole(1, pltpu.SMEM) + whole(12),
        out_specs=tuple(whole(3)),
        scratch_shapes=[
            pltpu.VMEM((2 * block, width), jnp.bfloat16),
            pltpu.VMEM((2 * block, 2 * w_in.shape[1]), jnp.float32),
            pltpu.VMEM((2 * block, 2 * heads * head_size), jnp.bfloat16),
        ],
        compiler_params=pltpu.CompilerParams(vmem_limit_bytes=16 * 1024 * 1024),
        cost_estimate=pl.CostEstimate(flops=4_000_000_000, bytes_accessed=3_000_000, transcendentals=400_000),
    )(
        local.astype(jnp.int32).reshape(1), stored(tokens), stored(same), stored(far_a), stored(far_b), gain, qk_gain,
        qk_gain2, w_vmem, w2_vmem, wo_vmem, wo2_vmem, projected,
    )
    to_far_a = send(third, back(FAR_A) + back(SAME))
    to_far_b = send(fourth, back(FAR_B))
    first, second = pl.pallas_call(
        output_kernel,
        out_shape=(row_block, row_block),
        in_specs=whole(3),
        out_specs=tuple(whole(2)),
        compiler_params=pltpu.CompilerParams(vmem_limit_bytes=8 * 1024 * 1024),
        cost_estimate=pl.CostEstimate(flops=600_000_000, bytes_accessed=1_000_000, transcendentals=0),
    )(joined, wo_vmem, wo2_vmem)
    to_near_b = send(second, back(NEAR_B))
    wide = lambda value: value.astype(jnp.float32)
    passed = (wide(first) + wide(jnp.where(local, to_far_a, to_far_b))).astype(jnp.bfloat16)
    to_near_a = send(passed, back(NEAR_A))
    kept = wide(tokens) + wide(jnp.where(local, fourth, to_far_a)) + wide(to_near_b)
    return (kept + wide(to_near_a)).astype(jnp.bfloat16)


def solution(mesh):
    return jax.shard_map(
        body,
        mesh=mesh,
        in_specs=(P(("dp", "mp"), None), P(), P(None, "mp"), P(None, "mp", None), P("mp", None)),
        out_specs=P(("dp", "mp"), None),
        check_vma=False,
    )
```

```python
import functools
import math

import jax
import jax.numpy as jnp
from jax import lax
from jax.experimental import pallas as pl
from jax.experimental.pallas import tpu as pltpu
from jax.sharding import PartitionSpec as P

EPSILON = 1e-06
CHIPS = 4
CORES = 2


def place(chip, core):
    return (chip % CHIPS) * CORES + core


NEAR_A = [
    (place(0, 0), place(1, 0)), (place(0, 1), place(3, 0)), (place(1, 0), place(0, 0)), (place(1, 1), place(2, 0)),
    (place(2, 0), place(3, 1)), (place(2, 1), place(1, 1)), (place(3, 0), place(2, 1)), (place(3, 1), place(0, 1)),
]
NEAR_B = [
    (place(0, 0), place(3, 0)), (place(0, 1), place(1, 0)), (place(1, 0), place(2, 0)), (place(1, 1), place(0, 0)),
    (place(2, 0), place(1, 1)), (place(2, 1), place(3, 1)), (place(3, 0), place(0, 1)), (place(3, 1), place(2, 1)),
]
SAME = [(place(0, 1), place(0, 0)), (place(1, 1), place(1, 0)), (place(2, 0), place(2, 1)), (place(3, 0), place(3, 1))]
FAR_A = [(place(1, 0), place(2, 0)), (place(0, 0), place(3, 0)), (place(3, 1), place(0, 1)), (place(2, 1), place(1, 1))]
FAR_B = [(place(3, 0), place(2, 0)), (place(2, 0), place(3, 0)), (place(1, 1), place(0, 1)), (place(0, 1), place(1, 1))]
SWAP = [(i, i ^ 1) for i in range(CHIPS * CORES)]
LOCAL = (place(0, 0), place(1, 0), place(2, 1), place(3, 1))


def back(pairs):
    return [(target, source) for source, target in pairs]


def send(value, pairs):
    return lax.ppermute(value, "mp", pairs)


def normalize(entries, gain):
    average = jnp.mean(entries, axis=-1, keepdims=True)
    centred = entries - average
    spread = jnp.mean(centred * centred, axis=-1, keepdims=True)
    return centred * lax.rsqrt(spread + EPSILON) * gain


def norm_rows(ref, gain_ref, normed, at):
    entries = ref[...].astype(jnp.float32)
    normed[at : at + ref.shape[0], :] = normalize(entries, gain_ref[...]).astype(jnp.bfloat16)


def normalize_heads(entries, gains, head_size):
    return jnp.concatenate(
        [
            normalize(entries[:, head * head_size : (head + 1) * head_size], gains[head : head + 1, :])
            for head in range(gains.shape[0])
        ],
        axis=1,
    ).astype(jnp.bfloat16)


def project_rows(rows, w_ref, qk_ref, at):
    heads, head_size = qk_ref.shape[1:]
    size = heads * head_size
    columns = slice(at, at + size)
    entries = jnp.dot(rows, w_ref[...], preferred_element_type=jnp.float32)
    return (
        columns,
        normalize_heads(entries[:, :size], qk_ref[0], head_size),
        normalize_heads(entries[:, size : 2 * size], qk_ref[1], head_size),
        entries[:, 2 * size :].astype(jnp.bfloat16),
    )


def attend(queries, keys, values, at, head_size, joined):
    for start in range(at, at + queries.shape[1] // 2, head_size):
        columns = slice(start, start + head_size)
        stacked = lambda refs: jnp.concatenate([ref[:, columns] for ref in refs], axis=0)
        scores = lax.dot_general(
            queries[:, columns], stacked(keys), (((1,), (1,)), ((), ())), preferred_element_type=jnp.float32
        ) * (1.0 / math.sqrt(head_size))
        raised = jnp.exp(scores - jnp.max(scores, axis=-1, keepdims=True))
        weights = (raised * (1.0 / jnp.sum(raised, axis=-1, keepdims=True))).astype(jnp.bfloat16)
        joined[:, columns] = jnp.dot(weights, stacked(values), preferred_element_type=jnp.float32).astype(jnp.bfloat16)


def out_terms(joined, w_ref, w2_ref, upper_ref, lower_ref):
    half, block = w_ref.shape[0], upper_ref.shape[0]
    for start in range(0, upper_ref.shape[1], 512):
        columns = slice(start, start + 512)
        term = jnp.dot(joined[:, :half], w_ref[:, columns], preferred_element_type=jnp.float32) + jnp.dot(
            joined[:, half:], w2_ref[:, columns], preferred_element_type=jnp.float32
        )
        upper_ref[:, columns] = term[:block].astype(jnp.bfloat16)
        lower_ref[:, columns] = term[block:].astype(jnp.bfloat16)


def first_kernel(a_ref, gain_ref, w_hbm, wo_hbm, normed, w_ref, wo_ref, sems):
    loads = [
        pltpu.make_async_copy(source, target, sems.at[i])
        for i, (source, target) in enumerate(((w_hbm, w_ref), (wo_hbm, wo_ref)))
    ]
    for load in loads:
        load.start()
    norm_rows(a_ref, gain_ref, normed, 0)
    for load in loads:
        load.wait()


def early_kernel(
    local_ref, own_ref, b_ref, same_ref, gain_ref, qk_ref, qk2_ref, w_ref, w2_ref, wo_ref, wo2_ref, near_ref,
    second_ref, third_ref, queries, near_keys, near_values, keys, values, normed, early, joined,
):
    block = own_ref.shape[0]
    heads, head_size = qk_ref.shape[1:]
    half = heads * head_size
    normed[:block, :] = near_ref[...]
    norm_rows(b_ref, gain_ref, normed, block)

    @pl.when(local_ref[0] == 1)
    def _():
        norm_rows(same_ref, gain_ref, normed, 2 * block)
        norm_rows(own_ref, gain_ref, normed, 3 * block)
        for at, qk, w in ((0, qk_ref, w_ref), (half, qk2_ref, w2_ref)):
            columns, some_queries, some_keys, some_values = project_rows(normed[...], w, qk, at)
            early[:, columns] = some_queries[block : 3 * block]
            queries[:block, columns] = some_queries[:block]
            queries[block:, columns] = some_queries[3 * block :]
            near_keys[:, columns] = some_keys[: 2 * block]
            keys[:, columns] = some_keys[2 * block :]
            near_values[:, columns] = some_values[: 2 * block]
            values[:, columns] = some_values[2 * block :]
            attend(early, (near_keys, keys), (near_values, values), at, head_size, joined)
        out_terms(joined, wo_ref, wo2_ref, second_ref, third_ref)

    @pl.when(local_ref[0] == 0)
    def _():
        for at, qk, w in ((0, qk_ref, w_ref), (half, qk2_ref, w2_ref)):
            columns, some_queries, some_keys, some_values = project_rows(normed[: 2 * block, :], w, qk, at)
            queries[:, columns] = some_queries
            near_keys[:, columns] = some_keys
            near_values[:, columns] = some_values


def far_kernel(
    local_ref, far_a_ref, far_b_ref, gain_ref, qk_ref, qk2_ref, w_ref, w2_ref, wo_ref, wo2_ref, near_keys, near_values,
    early_keys, early_values, third_ref, fourth_ref, keys, values, normed, queries, joined,
):
    block = far_a_ref.shape[0]
    heads, head_size = qk_ref.shape[1:]
    half = heads * head_size

    @pl.when(local_ref[0] == 1)
    def _():
        keys[...] = early_keys[...]
        values[...] = early_values[...]

    @pl.when(local_ref[0] == 0)
    def _():
        norm_rows(far_a_ref, gain_ref, normed, 0)
        norm_rows(far_b_ref, gain_ref, normed, block)
        for at, qk, w in ((0, qk_ref, w_ref), (half, qk2_ref, w2_ref)):
            columns, some_queries, some_keys, some_values = project_rows(normed[...], w, qk, at)
            queries[:, columns] = some_queries
            keys[:, columns] = some_keys
            values[:, columns] = some_values
            attend(queries, (near_keys, keys), (near_values, values), at, head_size, joined)
        out_terms(joined, wo_ref, wo2_ref, third_ref, fourth_ref)


def late_kernel(head_size, queries, near_keys, near_values, keys, values, wo_ref, wo2_ref, first_ref, other_ref, joined):
    half = wo_ref.shape[0]
    for at in (0, half):
        attend(queries, (near_keys, keys), (near_values, values), at, head_size, joined)
    out_terms(joined, wo_ref, wo2_ref, first_ref, other_ref)


def whole(count, space=pltpu.VMEM):
    return [pl.BlockSpec(memory_space=space)] * count


def held(value):
    return pltpu.with_memory_space_constraint(value, pltpu.VMEM)


def stored(value):
    return pltpu.with_memory_space_constraint(value, pltpu.HBM)


def body(tokens, ln_gain, w_in, qk_gain, w_out):
    block, width = tokens.shape
    heads, head_size = qk_gain.shape[1:]
    me = lax.axis_index("mp")
    local = (me // (CHIPS // 2 * CORES)) == (me % CORES)
    gain = ln_gain.reshape(1, width)

    near_a = send(tokens, NEAR_A)
    w_in2 = send(w_in, SWAP)
    w_out2 = send(w_out, SWAP)
    qk_gain2 = send(qk_gain, SWAP)
    same = send(tokens, SAME)
    near_b = send(tokens, NEAR_B)
    far_a = send(lax.optimization_barrier((near_a, same))[0], FAR_A)
    far_b = send(near_a, FAR_B)

    row_block = pltpu.VMEM((block, width), jnp.bfloat16)
    w2_vmem, wo2_vmem = held(w_in2), held(w_out2)
    normed, w_vmem, wo_vmem = pl.pallas_call(
        first_kernel,
        out_shape=(row_block, pltpu.VMEM(w_in.shape, jnp.bfloat16), pltpu.VMEM(w_out.shape, jnp.bfloat16)),
        in_specs=whole(2) + whole(2, pl.ANY),
        out_specs=tuple(whole(3)),
        scratch_shapes=[pltpu.SemaphoreType.DMA((2,))],
        compiler_params=pltpu.CompilerParams(vmem_limit_bytes=4 * 1024 * 1024),
        cost_estimate=pl.CostEstimate(flops=100000000000, bytes_accessed=10_000_000, transcendentals=0),
    )(held(near_a), gain, stored(w_in), stored(w_out))
    w_vmem, wo_vmem = held(w_vmem), held(wo_vmem)
    half_rows = pltpu.VMEM((2 * block, 2 * heads * head_size), jnp.bfloat16)
    half_normed = pltpu.VMEM((2 * block, width), jnp.bfloat16)
    flag = local.astype(jnp.int32).reshape(1)
    second, third, queries, near_keys, near_values, keys, values = pl.pallas_call(
        early_kernel,
        out_shape=(row_block, row_block) + (half_rows,) * 5,
        in_specs=whole(1, pltpu.SMEM) + whole(11),
        out_specs=tuple(whole(7)),
        scratch_shapes=[pltpu.VMEM((4 * block, width), jnp.bfloat16), half_rows, half_rows],
        compiler_params=pltpu.CompilerParams(vmem_limit_bytes=16 * 1024 * 1024),
        cost_estimate=pl.CostEstimate(flops=4_000_000_000, bytes_accessed=8_000_000, transcendentals=200_000),
    )(
        flag, held(tokens), held(near_b), held(same), gain, qk_gain, qk_gain2, w_vmem, w2_vmem, wo_vmem, wo2_vmem,
        held(normed),
    )
    to_near_b_early = send(second, [pair for pair in back(NEAR_B) if pair[0] in LOCAL])
    to_same = send(third, back(SAME))
    near_keys, near_values = held(near_keys), held(near_values)
    third, fourth, keys, values = pl.pallas_call(
        far_kernel,
        out_shape=(row_block, row_block, half_rows, half_rows),
        in_specs=whole(1, pltpu.SMEM) + whole(13),
        out_specs=tuple(whole(4)),
        scratch_shapes=[half_normed, half_rows, half_rows],
        compiler_params=pltpu.CompilerParams(vmem_limit_bytes=16 * 1024 * 1024),
        cost_estimate=pl.CostEstimate(flops=3_000_000_000, bytes_accessed=1_000_000, transcendentals=200_000),
    )(
        flag, held(far_a), held(far_b), gain, qk_gain, qk_gain2, w_vmem, w2_vmem, wo_vmem, wo2_vmem, near_keys,
        near_values, held(keys), held(values),
    )
    to_far_a = send(third, back(FAR_A))
    to_far_b = send(fourth, back(FAR_B))
    queries, to_near_b_early, to_same = lax.optimization_barrier((queries, to_near_b_early, to_same))
    first, other = pl.pallas_call(
        functools.partial(late_kernel, head_size),
        out_shape=(row_block, row_block),
        in_specs=whole(7),
        out_specs=tuple(whole(2)),
        scratch_shapes=[half_rows],
        compiler_params=pltpu.CompilerParams(vmem_limit_bytes=8 * 1024 * 1024),
        cost_estimate=pl.CostEstimate(flops=1_000_000_000, bytes_accessed=1_000_000, transcendentals=200_000),
    )(held(queries), near_keys, near_values, held(keys), held(values), wo_vmem, wo2_vmem)
    to_near_b = send(other, [pair for pair in back(NEAR_B) if pair[0] not in LOCAL])
    wide = lambda value: value.astype(jnp.float32)
    passed = (wide(first) + wide(jnp.where(local, to_far_a, to_far_b))).astype(jnp.bfloat16)
    to_near_a = send(passed, back(NEAR_A))
    kept = wide(tokens) + wide(jnp.where(local, other, to_same)) + wide(to_near_b) + wide(to_near_b_early)
    return (kept + wide(to_near_a)).astype(jnp.bfloat16)


def solution(mesh):
    return jax.shard_map(
        body,
        mesh=mesh,
        in_specs=(P(("dp", "mp"), None), P(), P(None, "mp"), P(None, "mp", None), P("mp", None)),
        out_specs=P(("dp", "mp"), None),
        check_vma=False,
    )
```

```python
import functools
import math

import jax
import jax.numpy as jnp
from jax import lax
from jax.experimental import pallas as pl
from jax.experimental.pallas import tpu as pltpu
from jax.sharding import PartitionSpec as P

EPSILON = 1e-06
CHIPS = 4
CORES = 2


def place(chip, core):
    return (chip % CHIPS) * CORES + core


NEAR_A = [
    (place(0, 0), place(1, 0)), (place(0, 1), place(3, 0)), (place(1, 0), place(0, 0)), (place(1, 1), place(2, 0)),
    (place(2, 0), place(3, 1)), (place(2, 1), place(1, 1)), (place(3, 0), place(2, 1)), (place(3, 1), place(0, 1)),
]
NEAR_B = [
    (place(0, 0), place(3, 0)), (place(0, 1), place(1, 0)), (place(1, 0), place(2, 0)), (place(1, 1), place(0, 0)),
    (place(2, 0), place(1, 1)), (place(2, 1), place(3, 1)), (place(3, 0), place(0, 1)), (place(3, 1), place(2, 1)),
]
SAME = [(place(0, 1), place(0, 0)), (place(1, 1), place(1, 0)), (place(2, 0), place(2, 1)), (place(3, 0), place(3, 1))]
FAR_A = [(place(1, 0), place(2, 0)), (place(0, 0), place(3, 0)), (place(3, 1), place(0, 1)), (place(2, 1), place(1, 1))]
FAR_B = [(place(3, 0), place(2, 0)), (place(2, 0), place(3, 0)), (place(1, 1), place(0, 1)), (place(0, 1), place(1, 1))]
SWAP = [(i, i ^ 1) for i in range(CHIPS * CORES)]
LOCAL = (place(0, 0), place(1, 0), place(2, 1), place(3, 1))


def back(pairs):
    return [(target, source) for source, target in pairs]


def send(value, pairs):
    return lax.ppermute(value, "mp", pairs)


def normalize(entries, gain):
    average = jnp.mean(entries, axis=-1, keepdims=True)
    centred = entries - average
    spread = jnp.mean(centred * centred, axis=-1, keepdims=True)
    return centred * lax.rsqrt(spread + EPSILON) * gain


def norm_rows(ref, gain_ref, normed, at):
    entries = ref[...].astype(jnp.float32)
    normed[at : at + ref.shape[0], :] = normalize(entries, gain_ref[...]).astype(jnp.bfloat16)


def normalize_heads(entries, gains, head_size):
    return jnp.concatenate(
        [
            normalize(entries[:, head * head_size : (head + 1) * head_size], gains[head : head + 1, :])
            for head in range(gains.shape[0])
        ],
        axis=1,
    ).astype(jnp.bfloat16)


def project_rows(rows, w_ref, qk_ref, at):
    heads, head_size = qk_ref.shape[1:]
    size = heads * head_size
    columns = slice(at, at + size)
    entries = jnp.dot(rows, w_ref[...], preferred_element_type=jnp.float32)
    return (
        columns,
        normalize_heads(entries[:, :size], qk_ref[0], head_size),
        normalize_heads(entries[:, size : 2 * size], qk_ref[1], head_size),
        entries[:, 2 * size :].astype(jnp.bfloat16),
    )


def attend(queries, keys, values, at, head_size, joined):
    for start in range(at, at + queries.shape[1] // 2, head_size):
        columns = slice(start, start + head_size)
        stacked = lambda refs: jnp.concatenate([ref[:, columns] for ref in refs], axis=0)
        scores = lax.dot_general(
            queries[:, columns], stacked(keys), (((1,), (1,)), ((), ())), preferred_element_type=jnp.float32
        ) * (1.0 / math.sqrt(head_size))
        raised = jnp.exp(scores - jnp.max(scores, axis=-1, keepdims=True))
        weights = (raised * (1.0 / jnp.sum(raised, axis=-1, keepdims=True))).astype(jnp.bfloat16)
        joined[:, columns] = jnp.dot(weights, stacked(values), preferred_element_type=jnp.float32).astype(jnp.bfloat16)


def out_terms(joined, w_ref, w2_ref, upper_ref, lower_ref):
    half, block = w_ref.shape[0], upper_ref.shape[0]
    for start in range(0, upper_ref.shape[1], 512):
        columns = slice(start, start + 512)
        term = jnp.dot(joined[:, :half], w_ref[:, columns], preferred_element_type=jnp.float32) + jnp.dot(
            joined[:, half:], w2_ref[:, columns], preferred_element_type=jnp.float32
        )
        upper_ref[:, columns] = term[:block].astype(jnp.bfloat16)
        lower_ref[:, columns] = term[block:].astype(jnp.bfloat16)


def first_kernel(a_ref, w_hbm, wo_hbm, w_ref, wo_ref, sems):
    loads = [
        pltpu.make_async_copy(source, target, sems.at[i])
        for i, (source, target) in enumerate(((w_hbm, w_ref), (wo_hbm, wo_ref)))
    ]
    for load in loads:
        load.start()
    for load in loads:
        load.wait()


def early_kernel(
    local_ref, own_ref, b_ref, same_ref, gain_ref, qk_ref, qk2_ref, w_ref, w2_ref, wo_ref, wo2_ref, near_ref,
    second_ref, third_ref, queries, near_keys, near_values, keys, values, normed, early, joined,
):
    block = own_ref.shape[0]
    heads, head_size = qk_ref.shape[1:]
    half = heads * head_size
    norm_rows(near_ref, gain_ref, normed, 0)
    norm_rows(b_ref, gain_ref, normed, block)

    @pl.when(local_ref[0] == 1)
    def _():
        norm_rows(same_ref, gain_ref, normed, 2 * block)
        norm_rows(own_ref, gain_ref, normed, 3 * block)
        for at, qk, w in ((0, qk_ref, w_ref), (half, qk2_ref, w2_ref)):
            columns, some_queries, some_keys, some_values = project_rows(normed[...], w, qk, at)
            early[:, columns] = some_queries[block : 3 * block]
            queries[:block, columns] = some_queries[:block]
            queries[block:, columns] = some_queries[3 * block :]
            near_keys[:, columns] = some_keys[: 2 * block]
            keys[:, columns] = some_keys[2 * block :]
            near_values[:, columns] = some_values[: 2 * block]
            values[:, columns] = some_values[2 * block :]
            attend(early, (near_keys, keys), (near_values, values), at, head_size, joined)
        out_terms(joined, wo_ref, wo2_ref, second_ref, third_ref)

    @pl.when(local_ref[0] == 0)
    def _():
        for at, qk, w in ((0, qk_ref, w_ref), (half, qk2_ref, w2_ref)):
            columns, some_queries, some_keys, some_values = project_rows(normed[: 2 * block, :], w, qk, at)
            queries[:, columns] = some_queries
            near_keys[:, columns] = some_keys
            near_values[:, columns] = some_values


def far_kernel(
    local_ref, far_a_ref, far_b_ref, gain_ref, qk_ref, qk2_ref, w_ref, w2_ref, wo_ref, wo2_ref, near_keys, near_values,
    early_keys, early_values, third_ref, fourth_ref, keys, values, normed, queries, joined,
):
    block = far_a_ref.shape[0]
    heads, head_size = qk_ref.shape[1:]
    half = heads * head_size

    @pl.when(local_ref[0] == 1)
    def _():
        keys[...] = early_keys[...]
        values[...] = early_values[...]

    @pl.when(local_ref[0] == 0)
    def _():
        norm_rows(far_a_ref, gain_ref, normed, 0)
        norm_rows(far_b_ref, gain_ref, normed, block)
        for at, qk, w in ((0, qk_ref, w_ref), (half, qk2_ref, w2_ref)):
            columns, some_queries, some_keys, some_values = project_rows(normed[...], w, qk, at)
            queries[:, columns] = some_queries
            keys[:, columns] = some_keys
            values[:, columns] = some_values
            attend(queries, (near_keys, keys), (near_values, values), at, head_size, joined)
        out_terms(joined, wo_ref, wo2_ref, third_ref, fourth_ref)


def late_kernel(head_size, queries, near_keys, near_values, keys, values, wo_ref, wo2_ref, first_ref, other_ref, joined):
    half = wo_ref.shape[0]
    for at in (0, half):
        attend(queries, (near_keys, keys), (near_values, values), at, head_size, joined)
    out_terms(joined, wo_ref, wo2_ref, first_ref, other_ref)


def whole(count, space=pltpu.VMEM):
    return [pl.BlockSpec(memory_space=space)] * count


def held(value):
    return pltpu.with_memory_space_constraint(value, pltpu.VMEM)


def stored(value):
    return pltpu.with_memory_space_constraint(value, pltpu.HBM)


def body(tokens, ln_gain, w_in, qk_gain, w_out):
    block, width = tokens.shape
    heads, head_size = qk_gain.shape[1:]
    me = lax.axis_index("mp")
    local = (me // (CHIPS // 2 * CORES)) == (me % CORES)
    gain = ln_gain.reshape(1, width)

    near_a = send(tokens, NEAR_A)
    w_in2 = send(w_in, SWAP)
    w_out2 = send(w_out, SWAP)
    qk_gain2 = send(qk_gain, SWAP)
    same = send(tokens, SAME)
    near_b = send(tokens, NEAR_B)
    far_a = send(lax.optimization_barrier((near_a, same))[0], FAR_A)
    far_b = send(near_a, FAR_B)

    row_block = pltpu.VMEM((block, width), jnp.bfloat16)
    w2_vmem, wo2_vmem = held(w_in2), held(w_out2)
    w_vmem, wo_vmem = pl.pallas_call(
        first_kernel,
        out_shape=(pltpu.VMEM(w_in.shape, jnp.bfloat16), pltpu.VMEM(w_out.shape, jnp.bfloat16)),
        in_specs=whole(1) + whole(2, pl.ANY),
        out_specs=tuple(whole(2)),
        scratch_shapes=[pltpu.SemaphoreType.DMA((2,))],
        compiler_params=pltpu.CompilerParams(vmem_limit_bytes=4 * 1024 * 1024),
        cost_estimate=pl.CostEstimate(flops=100000000000, bytes_accessed=10_000_000, transcendentals=0),
    )(held(near_a), stored(w_in), stored(w_out))
    w_vmem, wo_vmem = held(w_vmem), held(wo_vmem)
    half_rows = pltpu.VMEM((2 * block, 2 * heads * head_size), jnp.bfloat16)
    half_normed = pltpu.VMEM((2 * block, width), jnp.bfloat16)
    flag = local.astype(jnp.int32).reshape(1)
    second, third, queries, near_keys, near_values, keys, values = pl.pallas_call(
        early_kernel,
        out_shape=(row_block, row_block) + (half_rows,) * 5,
        in_specs=whole(1, pltpu.SMEM) + whole(11),
        out_specs=tuple(whole(7)),
        scratch_shapes=[pltpu.VMEM((4 * block, width), jnp.bfloat16), half_rows, half_rows],
        compiler_params=pltpu.CompilerParams(vmem_limit_bytes=16 * 1024 * 1024),
        cost_estimate=pl.CostEstimate(flops=4_000_000_000, bytes_accessed=8_000_000, transcendentals=200_000),
    )(
        flag, held(tokens), held(near_b), held(same), gain, qk_gain, qk_gain2, w_vmem, w2_vmem, wo_vmem, wo2_vmem,
        held(near_a),
    )
    to_near_b_early = send(second, [pair for pair in back(NEAR_B) if pair[0] in LOCAL])
    to_same = send(third, back(SAME))
    near_keys, near_values = held(near_keys), held(near_values)
    third, fourth, keys, values = pl.pallas_call(
        far_kernel,
        out_shape=(row_block, row_block, half_rows, half_rows),
        in_specs=whole(1, pltpu.SMEM) + whole(13),
        out_specs=tuple(whole(4)),
        scratch_shapes=[half_normed, half_rows, half_rows],
        compiler_params=pltpu.CompilerParams(vmem_limit_bytes=16 * 1024 * 1024),
        cost_estimate=pl.CostEstimate(flops=3_000_000_000, bytes_accessed=1_000_000, transcendentals=200_000),
    )(
        flag, held(far_a), held(far_b), gain, qk_gain, qk_gain2, w_vmem, w2_vmem, wo_vmem, wo2_vmem, near_keys,
        near_values, held(keys), held(values),
    )
    to_far_a = send(third, back(FAR_A))
    to_far_b = send(fourth, back(FAR_B))
    queries, to_near_b_early, to_same = lax.optimization_barrier((queries, to_near_b_early, to_same))
    first, other = pl.pallas_call(
        functools.partial(late_kernel, head_size),
        out_shape=(row_block, row_block),
        in_specs=whole(7),
        out_specs=tuple(whole(2)),
        scratch_shapes=[half_rows],
        compiler_params=pltpu.CompilerParams(vmem_limit_bytes=8 * 1024 * 1024),
        cost_estimate=pl.CostEstimate(flops=1_000_000_000, bytes_accessed=1_000_000, transcendentals=200_000),
    )(held(queries), near_keys, near_values, held(keys), held(values), wo_vmem, wo2_vmem)
    to_near_b = send(other, [pair for pair in back(NEAR_B) if pair[0] not in LOCAL])
    wide = lambda value: value.astype(jnp.float32)
    passed = (wide(first) + wide(jnp.where(local, to_far_a, to_far_b))).astype(jnp.bfloat16)
    to_near_a = send(passed, back(NEAR_A))
    kept = wide(tokens) + wide(jnp.where(local, other, to_same)) + wide(to_near_b) + wide(to_near_b_early)
    kept = lax.optimization_barrier(kept)
    return (kept + wide(to_near_a)).astype(jnp.bfloat16)


def solution(mesh):
    return jax.shard_map(
        body,
        mesh=mesh,
        in_specs=(P(("dp", "mp"), None), P(), P(None, "mp"), P(None, "mp", None), P("mp", None)),
        out_specs=P(("dp", "mp"), None),
        check_vma=False,
    )
```
